32 devices in a mesh: groups: 2 (over y), node: 4 (over x, core), peer: 4 (over z).
Axes of the slice: x: 2, y: 2, z: 4, core: 2. Of those that a mesh axis runs over, the one named last changes fastest.
Arguments:
- moe_rows: bfloat16 [128, 7168], P(('groups', 'node', 'peer')), parts along dimension 0, may hold values from -6 to 6
- route_nodes: int32 [128, 2], P(('groups', 'node', 'peer')), parts along dimension 0, may hold values from 0 to 3, all different within a row; in each aligned block of 4 rows (0 to 3, 4 to 7, ...) at most 3 rows name the same one
- gates: bfloat16 [128, 2, 2], P(('groups', 'node', 'peer')), parts along dimension 0, may hold values from 0.049804688 to 0.5
- w_gate: bfloat16 [8, 7168, 2048], P('node', None, 'peer'), may hold values from -0.0625 to 0.0625
- w_up: bfloat16 [8, 7168, 2048], P('node', None, 'peer'), may hold values from -0.0625 to 0.0625
- w_down: bfloat16 [8, 2048, 7168], P('node', 'peer'), may hold values from -0.125 to 0.125
Outputs:
- moe_out: bfloat16 [128, 7168], P(('groups', 'node', 'peer')), parts along dimension 0
The draws below stay inside these ranges and needn't reach their ends.
There are 2 independent parts, one for each index of `groups`. The reference program is written for one: setup_inputs(seed, part) draws one part's arguments, and reference() takes and returns one part's arrays. A program takes and returns all parts, laid end to end along the dimension named above; an argument that names none is the same for every part. Nothing has to cross between parts.
Inputs may be any that keep to these rules, and one draw needn't show every extreme that they name: `route_nodes`: each row names 2 different nodes; among the rows of one device no node is named by more than 3 rows, and in some devices' rows one node is named by exactly 3.
All inputs are finite; a program needn't handle non-finite values.
Results may differ from the reference program's by a relative error of at most 0.012.
Values may be sent and summed in bfloat16 or wider, within the bound.
A program may use at most 128 MiB of HBM per device.

```python
import math
import jax
import jax.numpy as jnp
import numpy as np
from jax import lax

D = 7168
FF = 2048
EXP_NODE = 2
ROWS_DEV = 4
NODES = 4
EXPERTS = 8
NODE_TOP = 2
CAP = 3
ROWS = 64
N_PEER = 4


def level_of(key, shape, pieces, smallest, largest):
    loudness = 1.0
    for dim, parts in pieces:
        draws = jax.random.uniform(jax.random.fold_in(jax.random.fold_in(key, 6), dim), (parts,), jnp.float32, smallest / len(pieces), largest / len(pieces))
        loudness = loudness * jnp.repeat(jnp.exp(draws), shape[dim] // parts).reshape((-1,) + (1,) * (len(shape) - 1 - dim))
    return loudness


def routed_block(key, own, number, rows, count, top, reach, slope):
    order = jax.random.permutation(key, count)
    heavy_load, common = shares(count, rows * top, reach, slope, True), shares(count, rows * top, reach, slope, False)
    places = jnp.arange(count)

    def named(lengths, turn):
        used = int((lengths > 0).sum())
        fixed = max(1, used // 4)
        passed = fixed + (places - fixed + turn * (used - fixed)) % max(1, count - fixed)
        return jnp.zeros((count,), jnp.int32).at[order[jnp.where(places < fixed, places, passed)]].set(jnp.asarray(lengths, jnp.int32))

    lengths = jnp.where(number % 4 == 0, named(heavy_load, number // 4), named(common, number - number // 4 - 1))
    mixed = jax.random.permutation(jax.random.fold_in(own, 3), count)
    donor, receiver = mixed[0:count // 2 * 2:2], mixed[1:count // 2 * 2:2]
    margin = jnp.minimum(lengths[donor] - 1, reach - lengths[receiver]) // 2
    margin = jnp.where((donor == order[0]) | (receiver == order[0]) | (lengths[receiver] == 0), 0, jnp.maximum(margin, 0))
    passed = jax.random.randint(jax.random.fold_in(own, 4), (count // 2,), 0, 1 << 20) % (margin + 1)
    lengths = lengths.at[donor].add(-passed).at[receiver].add(passed)
    labels = jnp.searchsorted(jnp.cumsum(lengths), jnp.arange(rows * top), side="right").astype(jnp.int32)
    listing = labels.reshape(top, rows).T
    listing = listing[jax.random.permutation(jax.random.fold_in(own, 1), rows)]
    turn = jax.random.randint(jax.random.fold_in(own, 2), (rows, 1), 0, top)
    return jnp.take_along_axis(listing, (jnp.arange(top)[None, :] + turn) % top, axis=1)


def shares(count, total, bound, lean, full):
    loads = [(1 << 20) // math.isqrt(rank ** lean) + 1 for rank in range(1, count + 1)]
    largest = bound if full else min(bound, max(-(-total // count), total * loads[0] // sum(loads)))
    least = 1 if total - largest >= count - 1 else 0
    given, rest = [largest] + [least] * (count - 1), total - largest - least * (count - 1)
    while rest > 0:
        candidates = [i for i in range(1, count) if given[i] < largest] or [i for i in range(1, count) if given[i] < bound]
        whole, left = sum([loads[i] for i in candidates]), rest
        for i in candidates:
            addition = min(bound - given[i], max(1, left * loads[i] // whole), rest)
            given[i] = given[i] + addition
            rest = rest - addition
    return np.array(given)


def noise(stream_key, shape, scale, bound, split=(), kind=jnp.bfloat16):
    factor_of = level_of(stream_key, shape, split, -0.22, 0.18) if split else 1.0
    drawn = jax.random.normal(stream_key, shape, jnp.float32) * scale * factor_of
    return jnp.minimum(jnp.maximum(drawn, -bound), bound).astype(kind)


def setup_inputs(seed: int = 0, part: int = 0) -> dict:
    splits = jax.random.split(jax.random.key(seed), 7)
    part_splits = jax.random.split(jax.random.fold_in(splits[6], part), 7)
    moe_rows = noise(part_splits[0], (ROWS, D), 1.0, 6.0, ((0, 16),))
    route_nodes_keys = jax.random.split(jax.random.fold_in(part_splits[1], 1), ROWS // ROWS_DEV)
    route_nodes_turns = jax.random.permutation(jax.random.fold_in(part_splits[1], 3), ROWS // ROWS_DEV)
    route_nodes = jax.vmap(lambda own, number: routed_block(jax.random.fold_in(part_splits[1], 2), own, number, ROWS_DEV, NODES, NODE_TOP, CAP, 2))(route_nodes_keys, route_nodes_turns).reshape((ROWS, NODE_TOP))
    gates = jnp.clip(jnp.exp(math.log(0.5) - 2.306499 * jax.random.uniform(part_splits[2], (ROWS, NODE_TOP, EXP_NODE), jnp.float32) ** level_of(part_splits[2], (ROWS, NODE_TOP, EXP_NODE), ((0, 16),), -0.2, 0.2)), 0.049804688, 0.5).astype(jnp.bfloat16)
    w_gate = noise(splits[3], (EXPERTS, D, FF), D ** -0.5, 0.0625, ((0, 4), (2, 4)))
    w_up = noise(splits[4], (EXPERTS, D, FF), D ** -0.5, 0.0625, ((0, 4), (2, 4)))
    w_down = noise(splits[5], (EXPERTS, FF, D), FF ** -0.5, 0.125, ((0, 4), (1, 4)))
    return {"moe_rows": moe_rows, "route_nodes": route_nodes, "gates": gates, "w_gate": w_gate, "w_up": w_up, "w_down": w_down}


def reference(moe_rows, route_nodes, gates, w_gate, w_up, w_down):
    block_size = FF // N_PEER
    zero_index = jnp.int32(0)
    gate_values = gates.astype(jnp.float32)

    def node_term(carry, node_index):
        hit_mask = (route_nodes == node_index).astype(jnp.float32)
        node_gates = jnp.einsum('rj,rje->re', hit_mask, gate_values)

        def block_term(inner, block_index):
            start = (block_index * block_size).astype(jnp.int32)
            accumulated = jnp.zeros(moe_rows.shape, jnp.float32)
            for expert_slot in range(EXP_NODE):
                expert = (node_index * EXP_NODE + expert_slot).astype(jnp.int32)
                gate_block = lax.dynamic_slice(w_gate, (expert, zero_index, start), (1, D, block_size))[0]
                up_block = lax.dynamic_slice(w_up, (expert, zero_index, start), (1, D, block_size))[0]
                down_block = lax.dynamic_slice(w_down, (expert, start, zero_index), (1, block_size, D))[0]
                gate_proj = jnp.dot(moe_rows, gate_block, preferred_element_type=jnp.float32)
                up_proj = jnp.dot(moe_rows, up_block, preferred_element_type=jnp.float32)
                hidden = (jax.nn.silu(gate_proj) * up_proj).astype(jnp.bfloat16)
                projected = jnp.dot(hidden, down_block, preferred_element_type=jnp.float32)
                accumulated = accumulated + node_gates[:, expert_slot:expert_slot + 1] * projected
            rounded = lax.optimization_barrier(accumulated.astype(jnp.bfloat16))
            return inner + rounded.astype(jnp.float32), None

        node_sum, _ = lax.scan(block_term, jnp.zeros(moe_rows.shape, jnp.float32), jnp.arange(N_PEER, dtype=jnp.int32))
        rounded_node = lax.optimization_barrier(node_sum.astype(jnp.bfloat16))
        return carry + rounded_node.astype(jnp.float32), None

    combined, _ = lax.scan(node_term, jnp.zeros(moe_rows.shape, jnp.float32), jnp.arange(NODES, dtype=jnp.int32))
    return combined.astype(jnp.bfloat16)
```

```python
import functools

import jax
import jax.numpy as jnp
from jax import lax
from jax.experimental import pallas as pl
from jax.experimental.pallas import tpu as pltpu
from jax.sharding import PartitionSpec as P

MESH = pl.DeviceIdType.MESH
EXP_NODE = 2
CORES = 2
SLOT = 16
GATE_COLS = 128
CHUNKS_IN = 2
CHUNKS_OUT = 2
F32 = jnp.float32
BF16 = jnp.bfloat16


def kernel(
    peers, xs, rows, chunks_in, chunks_out,
    x_ref, g_ref, wg_hbm, wu_hbm, wd_hbm, out_ref,
    wg, wu, wd, zin, gin, zgate, ggate, acc, hid,
    part, cbuf, xsum, xbuf, zout, zbuf,
    w_sem, d_sem,
    zs, zr, xs_s, xs_r, cs, cr,
    gzs, gzr, gxs, gxr, gcs, gcr,
    ocs, ocr, oxs, oxr, ozs, ozr,
):
    width = x_ref.shape[1]
    pieces = SLOT // rows
    node_rows = peers * rows
    node = lax.axis_index("node")
    p = lax.axis_index("peer")
    c = lax.rem(node, CORES)
    xi = lax.div(node, CORES)

    w_in = width // chunks_in
    v_in = w_in // pieces
    w_out = width // chunks_out
    v_out = w_out // pieces

    weight_copies = []
    for t in range(chunks_in):
        both = []
        for i, (src, dst) in enumerate(((wg_hbm, wg), (wu_hbm, wu))):
            span = pl.ds(t * w_in, w_in)
            copy = pltpu.make_async_copy(src.at[:, span, :], dst.at[:, span, :], w_sem.at[t, i])
            copy.start()
            both.append(copy)
        weight_copies.append(both)
    down_copies = []
    for t in range(chunks_out):
        span = pl.ds(t * w_out, w_out)
        copy = pltpu.make_async_copy(wd_hbm.at[:, :, span], wd.at[:, :, span], d_sem.at[t])
        copy.start()
        down_copies.append(copy)

    def peer_of(d):
        return lax.rem(p + d, peers)

    def x_of(d):
        return lax.rem(xi + d, xs)

    barrier = pltpu.get_barrier_semaphore()
    for d in range(1, peers):
        pl.semaphore_signal(barrier, inc=1, device_id={"peer": peer_of(d)}, device_id_type=MESH)
    for d in range(1, xs):
        pl.semaphore_signal(
            barrier, inc=1, device_id={"node": x_of(d) * CORES + c}, device_id_type=MESH
        )
    pl.semaphore_signal(
        barrier, inc=1, device_id={"node": xi * CORES + 1 - c}, device_id_type=MESH
    )

    for t in range(chunks_in):
        own = [
            x_ref[:, t * w_in + j * v_in : t * w_in + (j + 1) * v_in].astype(F32)
            for j in range(pieces)
        ]
        zin[t, p] = jnp.concatenate(own, axis=0).astype(BF16)
    zgate[p] = jnp.concatenate([g_ref[...]] * pieces, axis=0).astype(BF16)

    pl.semaphore_wait(barrier, peers - 1 + xs - 1 + 1)

    sends = []

    def send(src, dst, ssem, rsem, where):
        copy = pltpu.make_async_remote_copy(
            src_ref=src, dst_ref=dst, send_sem=ssem, recv_sem=rsem,
            device_id=where, device_id_type=MESH,
        )
        copy.start()
        sends.append(copy)

    def arrived(dst, ssem, rsem, where):
        pltpu.make_async_remote_copy(
            src_ref=dst, dst_ref=dst, send_sem=ssem, recv_sem=rsem,
            device_id=where, device_id_type=MESH,
        ).wait_recv()

    def to_peer(d):
        return {"peer": peer_of(d)}

    def to_x(d):
        return {"node": x_of(d) * CORES + c}

    to_core = {"node": xi * CORES + 1 - c}

    for t in range(chunks_in):
        for d in range(1, peers):
            send(zin.at[t, p], zin.at[t, p], zs.at[t, d - 1], zr.at[t, d - 1], to_peer(d))
    for d in range(1, peers):
        send(zgate.at[p], zgate.at[p], gzs.at[d - 1], gzr.at[d - 1], to_peer(d))

    row_at = lax.broadcasted_iota(jnp.int32, (node_rows, peers * SLOT), 0)
    col_at = lax.broadcasted_iota(jnp.int32, (node_rows, peers * SLOT), 1)
    row_base = (row_at // rows) * SLOT + row_at % rows

    def spread(j):
        return jnp.where(col_at == row_base + j * rows, 1.0, 0.0).astype(BF16)

    def place(t):
        for d in range(1, peers):
            arrived(zin.at[t, peer_of(peers - d)], zs.at[t, d - 1], zr.at[t, d - 1], to_peer(d))
        stacked = zin[t].reshape(peers * SLOT, v_in)
        for j in range(pieces):
            gin[t, c, xi, :, j * v_in : (j + 1) * v_in] = jnp.dot(
                spread(j), stacked, preferred_element_type=F32
            ).astype(BF16)
        for d in range(1, xs):
            send(gin.at[t, c, xi], gin.at[t, c, xi], xs_s.at[t, d - 1], xs_r.at[t, d - 1], to_x(d))
        send(gin.at[t, c, xi], gin.at[t, c, xi], cs.at[t, 0], cr.at[t, 0], to_core)

    def forward(t):
        for d in range(1, xs):
            other = x_of(xs - d)
            block = gin.at[t, c, other]
            arrived(block, xs_s.at[t, d - 1], xs_r.at[t, d - 1], to_x(d))
            send(block, block, cs.at[t, d], cr.at[t, d], to_core)

    def gathered(t):
        for d in range(xs):
            block = gin.at[t, 1 - c, x_of(xs - d)]
            arrived(block, cs.at[t, d], cr.at[t, d], to_core)

    all_rows = CORES * xs * node_rows

    def first_half(t):
        gathered(t)
        for copy in weight_copies[t]:
            copy.wait()
        lhs = gin[t].reshape(all_rows, w_in)
        for e in range(EXP_NODE):
            for i, w in enumerate((wg, wu)):
                value = jnp.dot(
                    lhs, w[e, t * w_in : (t + 1) * w_in, :], preferred_element_type=F32
                )
                if t == 0:
                    acc[e, i] = value
                else:
                    acc[e, i] += value

    for t in range(chunks_in):
        place(t)

    for d in range(1, peers):
        arrived(zgate.at[peer_of(peers - d)], gzs.at[d - 1], gzr.at[d - 1], to_peer(d))
    ggate[c, xi] = jnp.dot(
        spread(0), zgate[...].reshape(peers * SLOT, GATE_COLS), preferred_element_type=F32
    ).astype(BF16)
    own_gates = ggate.at[c, xi]
    for d in range(1, xs):
        send(own_gates, own_gates, gxs.at[d - 1], gxr.at[d - 1], to_x(d))
    send(own_gates, own_gates, gcs.at[0], gcr.at[0], to_core)

    forward(0)
    for t in range(chunks_in):
        if t + 1 < chunks_in:
            forward(t + 1)
        else:
            for d in range(1, xs):
                block = ggate.at[c, x_of(xs - d)]
                arrived(block, gxs.at[d - 1], gxr.at[d - 1], to_x(d))
                send(block, block, gcs.at[d], gcr.at[d], to_core)
        first_half(t)

    for d in range(xs):
        arrived(ggate.at[1 - c, x_of(xs - d)], gcs.at[d], gcr.at[d], to_core)
    every_gate = ggate[...].reshape(all_rows, GATE_COLS).astype(F32)
    gate_col = lax.broadcasted_iota(jnp.int32, (all_rows, GATE_COLS), 1)
    row_gates = []
    for e in range(EXP_NODE):
        picked = jnp.where(gate_col == node * EXP_NODE + e, every_gate, 0.0)
        row_gates.append(jnp.sum(picked, axis=1, keepdims=True))
        gate_proj = acc[e, 0]
        hid[e] = (gate_proj / (1.0 + jnp.exp(-gate_proj)) * acc[e, 1]).astype(BF16)

    def second_half(t):
        down_copies[t].wait()
        total = None
        for e in range(EXP_NODE):
            value = row_gates[e] * jnp.dot(
                hid[e], wd[e, :, t * w_out : (t + 1) * w_out], preferred_element_type=F32
            )
            total = value if total is None else total + value
        part[t] = total.astype(BF16).reshape(CORES, xs, node_rows, w_out)
        send(part.at[t, 1 - c], cbuf.at[t], ocs.at[t], ocr.at[t], to_core)

    def core_sum(t):
        arrived(cbuf.at[t], ocs.at[t], ocr.at[t], to_core)
        xsum[t] = (part[t, c].astype(F32) + cbuf[t].astype(F32)).astype(BF16)
        for d in range(1, xs):
            send(
                xsum.at[t, x_of(d)], xbuf.at[t, d - 1],
                oxs.at[t, d - 1], oxr.at[t, d - 1], to_x(d),
            )

    row_of = lax.broadcasted_iota(jnp.int32, (peers * SLOT, node_rows), 1)
    slot_of = lax.broadcasted_iota(jnp.int32, (peers * SLOT, node_rows), 0)
    slot_base = (row_of // rows) * SLOT + row_of % rows

    def node_sum(t):
        value = xsum[t, xi].astype(F32)
        for d in range(1, xs):
            arrived(xbuf.at[t, d - 1], oxs.at[t, d - 1], oxr.at[t, d - 1], to_x(d))
            value = value + xbuf[t, d - 1].astype(F32)
        value = value.astype(BF16)
        slots = None
        for j in range(pieces):
            gather = jnp.where(slot_of == slot_base + j * rows, 1.0, 0.0).astype(BF16)
            piece = jnp.dot(
                gather, value[:, j * v_out : (j + 1) * v_out], preferred_element_type=F32
            )
            slots = piece if slots is None else slots + piece
        zout[t] = slots.astype(BF16).reshape(peers, SLOT, v_out)
        for d in range(1, peers):
            send(
                zout.at[t, peer_of(d)], zbuf.at[t, d - 1],
                ozs.at[t, d - 1], ozr.at[t, d - 1], to_peer(d),
            )

    def finish(t):
        value = zout[t, p].astype(F32)
        for d in range(1, peers):
            arrived(zbuf.at[t, d - 1], ozs.at[t, d - 1], ozr.at[t, d - 1], to_peer(d))
            value = value + zbuf[t, d - 1].astype(F32)
        for j in range(pieces):
            out_ref[:, t * w_out + j * v_out : t * w_out + (j + 1) * v_out] = value[
                j * rows : (j + 1) * rows
            ].astype(BF16)

    steps = (second_half, core_sum, node_sum, finish)
    for t in range(chunks_out + len(steps) - 1):
        for lag, step in enumerate(steps):
            if 0 <= t - lag < chunks_out:
                step(t - lag)

    for copy in sends:
        copy.wait_send()


def on_device(moe_rows, route_nodes, gates, w_gate, w_up, w_down):
    node_count = lax.axis_size("node")
    peers = lax.axis_size("peer")
    xs = node_count // CORES
    rows, width = moe_rows.shape
    hidden = w_gate.shape[2]
    pieces = SLOT // rows
    node_rows = peers * rows
    all_rows = node_count * node_rows
    ti, to = CHUNKS_IN, CHUNKS_OUT
    wi, wo = width // ti, width // to
    vi, vo = wi // pieces, wo // pieces

    column = jnp.arange(GATE_COLS, dtype=jnp.int32)[None, :]
    gate_matrix = jnp.zeros((rows, GATE_COLS), F32)
    for j in range(route_nodes.shape[1]):
        for e in range(EXP_NODE):
            hit = column == route_nodes[:, j : j + 1] * EXP_NODE + e
            gate_matrix = jnp.where(hit, gates[:, j, e : e + 1].astype(F32), gate_matrix)

    vmem = pl.BlockSpec(memory_space=pltpu.VMEM)
    hbm = pl.BlockSpec(memory_space=pl.ANY)
    dma = pltpu.SemaphoreType.DMA
    far = max(peers - 1, 1)
    xfar = max(xs - 1, 1)
    scratch = [
        pltpu.VMEM(w_gate.shape, BF16),
        pltpu.VMEM(w_up.shape, BF16),
        pltpu.VMEM(w_down.shape, BF16),
        pltpu.VMEM((ti, peers, SLOT, vi), BF16),
        pltpu.VMEM((ti, CORES, xs, node_rows, wi), BF16),
        pltpu.VMEM((peers, SLOT, GATE_COLS), BF16),
        pltpu.VMEM((CORES, xs, node_rows, GATE_COLS), BF16),
        pltpu.VMEM((EXP_NODE, 2, all_rows, hidden), F32),
        pltpu.VMEM((EXP_NODE, all_rows, hidden), BF16),
        pltpu.VMEM((to, CORES, xs, node_rows, wo), BF16),
        pltpu.VMEM((to, xs, node_rows, wo), BF16),
        pltpu.VMEM((to, xs, node_rows, wo), BF16),
        pltpu.VMEM((to, xfar, node_rows, wo), BF16),
        pltpu.VMEM((to, peers, SLOT, vo), BF16),
        pltpu.VMEM((to, far, SLOT, vo), BF16),
        dma((ti, 2)), dma((to,)),
        dma((ti, far)), dma((ti, far)), dma((ti, xfar)), dma((ti, xfar)),
        dma((ti, xs)), dma((ti, xs)),
        dma((far,)), dma((far,)), dma((xfar,)), dma((xfar,)), dma((xs,)), dma((xs,)),
        dma((to,)), dma((to,)), dma((to, xfar)), dma((to, xfar)), dma((to, far)), dma((to, far)),
    ]
    weight_count = w_gate.size + w_up.size + w_down.size
    return pl.pallas_call(
        functools.partial(kernel, peers, xs, rows, ti, to),
        out_shape=jax.ShapeDtypeStruct((rows, width), BF16),
        in_specs=[vmem, vmem, hbm, hbm, hbm],
        out_specs=vmem,
        scratch_shapes=scratch,
        compiler_params=pltpu.CompilerParams(
            collective_id=0, has_side_effects=True, vmem_limit_bytes=60 * 1024 * 1024
        ),
        cost_estimate=pl.CostEstimate(
            flops=2 * all_rows * weight_count,
            bytes_accessed=2 * weight_count,
            transcendentals=EXP_NODE * all_rows * hidden,
        ),
    )(moe_rows, gate_matrix, w_gate, w_up, w_down)


def solution(mesh):
    in_specs = (
        P(("groups", "node", "peer"), None),
        P(("groups", "node", "peer"), None),
        P(("groups", "node", "peer"), None, None),
        P("node", None, "peer"),
        P("node", None, "peer"),
        P("node", "peer", None),
    )
    out_specs = P(("groups", "node", "peer"), None)
    return jax.shard_map(
        on_device, mesh=mesh, in_specs=in_specs, out_specs=out_specs, check_vma=False
    )
```

```python
import functools

import jax
import jax.numpy as jnp
from jax import lax
from jax.experimental import pallas as pl
from jax.experimental.pallas import tpu as pltpu
from jax.sharding import PartitionSpec as P

MESH = pl.DeviceIdType.MESH
EXP_NODE = 2
CORES = 2
SLOT = 16
GATE_COLS = 128
UNIT = 512
PARTS_IN = 4
PARTS_OUT = 4
LAGS = (0, 1, 3, 5)
F32 = jnp.float32
BF16 = jnp.bfloat16


def chunks_of(width, parts):
    units = width // UNIT
    parts = min(parts, units)
    edges = [UNIT * (units * k // parts) for k in range(parts + 1)]
    return [(a, b - a) for a, b in zip(edges[:-1], edges[1:])]


def kernel(
    peers, xs, rows, spans_in, spans_out,
    x_ref, r_ref, g_ref, wg_hbm, wu_hbm, wd_hbm, out_ref,
    wg, wu, wd, zins, gins, zgate, ggate, acc, hid,
    parts, cbufs, xsums, xbufs, zouts, zbufs,
    w_sem, d_sem,
    zs, zr, xs_s, xs_r, cs, cr,
    gzs, gzr, gxs, gxr, gcs, gcr,
    ocs, ocr, oxs, oxr, ozs, ozr,
):
    chunks_in, chunks_out = len(spans_in), len(spans_out)
    pieces = SLOT // rows
    node_rows = peers * rows
    node = lax.axis_index("node")
    p = lax.axis_index("peer")
    c = lax.rem(node, CORES)
    xi = lax.div(node, CORES)

    weight_copies = []
    for t in range(chunks_in):
        both = []
        for i, (src, dst) in enumerate(((wg_hbm, wg), (wu_hbm, wu))):
            span = pl.ds(*spans_in[t])
            copy = pltpu.make_async_copy(src.at[:, span, :], dst.at[:, span, :], w_sem.at[t, i])
            copy.start()
            both.append(copy)
        weight_copies.append(both)
    down_copies = []
    for t in range(chunks_out):
        span = pl.ds(*spans_out[t])
        copy = pltpu.make_async_copy(wd_hbm.at[:, :, span], wd.at[:, :, span], d_sem.at[t])
        copy.start()
        down_copies.append(copy)

    def peer_of(d):
        return lax.rem(p + d, peers)

    def x_of(d):
        return lax.rem(xi + d, xs)

    barrier = pltpu.get_barrier_semaphore()
    for d in range(1, peers):
        pl.semaphore_signal(barrier, inc=1, device_id={"peer": peer_of(d)}, device_id_type=MESH)
    for d in range(1, xs):
        pl.semaphore_signal(
            barrier, inc=1, device_id={"node": x_of(d) * CORES + c}, device_id_type=MESH
        )
    pl.semaphore_signal(
        barrier, inc=1, device_id={"node": xi * CORES + 1 - c}, device_id_type=MESH
    )

    for t in range(chunks_in):
        at, w_in = spans_in[t]
        v_in = w_in // pieces
        own = [
            x_ref[:, at + j * v_in : at + (j + 1) * v_in].astype(F32) for j in range(pieces)
        ]
        zins[t][p] = jnp.concatenate(own, axis=0).astype(BF16)
    column = lax.broadcasted_iota(jnp.int32, (1, GATE_COLS), 1)
    gate_rows = []
    for r in range(rows):
        line = jnp.zeros((1, GATE_COLS), F32)
        values = g_ref[r].astype(F32)
        for j in range(r_ref.shape[1]):
            for e in range(EXP_NODE):
                hit = column == r_ref[r : r + 1, j : j + 1] * EXP_NODE + e
                line = jnp.where(hit, values[j : j + 1, e : e + 1], line)
        gate_rows.append(line)
    zgate[p] = jnp.concatenate(gate_rows * pieces, axis=0).astype(BF16)

    pl.semaphore_wait(barrier, peers - 1 + xs - 1 + 1)

    sends = []

    def send(src, dst, ssem, rsem, where):
        copy = pltpu.make_async_remote_copy(
            src_ref=src, dst_ref=dst, send_sem=ssem, recv_sem=rsem,
            device_id=where, device_id_type=MESH,
        )
        copy.start()
        sends.append(copy)

    def arrived(dst, ssem, rsem, where):
        pltpu.make_async_remote_copy(
            src_ref=dst, dst_ref=dst, send_sem=ssem, recv_sem=rsem,
            device_id=where, device_id_type=MESH,
        ).wait_recv()

    def to_peer(d):
        return {"peer": peer_of(d)}

    def to_x(d):
        return {"node": x_of(d) * CORES + c}

    to_core = {"node": xi * CORES + 1 - c}

    for t in range(chunks_in):
        for d in range(1, peers):
            send(zins[t].at[p], zins[t].at[p], zs.at[t, d - 1], zr.at[t, d - 1], to_peer(d))
    for d in range(1, peers):
        send(zgate.at[p], zgate.at[p], gzs.at[d - 1], gzr.at[d - 1], to_peer(d))

    row_at = lax.broadcasted_iota(jnp.int32, (node_rows, peers * SLOT), 0)
    col_at = lax.broadcasted_iota(jnp.int32, (node_rows, peers * SLOT), 1)
    row_base = (row_at // rows) * SLOT + row_at % rows

    def spread(j):
        return jnp.where(col_at == row_base + j * rows, 1.0, 0.0).astype(BF16)

    def place(t):
        for d in range(1, peers):
            arrived(zins[t].at[peer_of(peers - d)], zs.at[t, d - 1], zr.at[t, d - 1], to_peer(d))
        gin = gins[t]
        v_in = spans_in[t][1] // pieces
        stacked = zins[t][...].reshape(peers * SLOT, v_in)
        for j in range(pieces):
            gin[c, xi, :, j * v_in : (j + 1) * v_in] = jnp.dot(
                spread(j), stacked, preferred_element_type=F32
            ).astype(BF16)
        for d in range(1, xs):
            send(gin.at[c, xi], gin.at[c, xi], xs_s.at[t, d - 1], xs_r.at[t, d - 1], to_x(d))
        send(gin.at[c, xi], gin.at[c, xi], cs.at[t, 0], cr.at[t, 0], to_core)

    def forward(t):
        for d in range(1, xs):
            other = x_of(xs - d)
            block = gins[t].at[c, other]
            arrived(block, xs_s.at[t, d - 1], xs_r.at[t, d - 1], to_x(d))
            send(block, block, cs.at[t, d], cr.at[t, d], to_core)

    def gathered(t):
        for d in range(xs):
            block = gins[t].at[1 - c, x_of(xs - d)]
            arrived(block, cs.at[t, d], cr.at[t, d], to_core)

    all_rows = CORES * xs * node_rows

    def first_half(t):
        gathered(t)
        for copy in weight_copies[t]:
            copy.wait()
        at, w_in = spans_in[t]
        lhs = gins[t][...].reshape(all_rows, w_in)
        for e in range(EXP_NODE):
            for i, w in enumerate((wg, wu)):
                value = jnp.dot(
                    lhs, w[e, at : at + w_in, :], preferred_element_type=F32
                )
                if t == 0:
                    acc[e, i] = value
                else:
                    acc[e, i] += value

    for t in range(chunks_in):
        place(t)

    for d in range(1, peers):
        arrived(zgate.at[peer_of(peers - d)], gzs.at[d - 1], gzr.at[d - 1], to_peer(d))
    ggate[c, xi] = jnp.dot(
        spread(0), zgate[...].reshape(peers * SLOT, GATE_COLS), preferred_element_type=F32
    ).astype(BF16)
    own_gates = ggate.at[c, xi]
    for d in range(1, xs):
        send(own_gates, own_gates, gxs.at[d - 1], gxr.at[d - 1], to_x(d))
    send(own_gates, own_gates, gcs.at[0], gcr.at[0], to_core)

    forward(0)
    for t in range(chunks_in):
        if t + 1 < chunks_in:
            forward(t + 1)
        else:
            for d in range(1, xs):
                block = ggate.at[c, x_of(xs - d)]
                arrived(block, gxs.at[d - 1], gxr.at[d - 1], to_x(d))
                send(block, block, gcs.at[d], gcr.at[d], to_core)
        first_half(t)

    for d in range(xs):
        arrived(ggate.at[1 - c, x_of(xs - d)], gcs.at[d], gcr.at[d], to_core)
    every_gate = ggate[...].reshape(all_rows, GATE_COLS).astype(F32)
    gate_col = lax.broadcasted_iota(jnp.int32, (all_rows, GATE_COLS), 1)
    row_gates = []
    for e in range(EXP_NODE):
        picked = jnp.where(gate_col == node * EXP_NODE + e, every_gate, 0.0)
        row_gates.append(jnp.sum(picked, axis=1, keepdims=True))
        gate_proj = acc[e, 0]
        hid[e] = (gate_proj / (1.0 + jnp.exp(-gate_proj)) * acc[e, 1]).astype(BF16)

    def second_half(t):
        down_copies[t].wait()
        total = None
        at, w_out = spans_out[t]
        for e in range(EXP_NODE):
            value = row_gates[e] * jnp.dot(
                hid[e], wd[e, :, at : at + w_out], preferred_element_type=F32
            )
            total = value if total is None else total + value
        parts[t][...] = total.astype(BF16).reshape(CORES, xs, node_rows, w_out)
        send(parts[t].at[1 - c], cbufs[t], ocs.at[t], ocr.at[t], to_core)

    def core_sum(t):
        arrived(cbufs[t], ocs.at[t], ocr.at[t], to_core)
        xsums[t][...] = (parts[t][c].astype(F32) + cbufs[t][...].astype(F32)).astype(BF16)
        for d in range(1, xs):
            send(
                xsums[t].at[x_of(d)], xbufs[t].at[d - 1],
                oxs.at[t, d - 1], oxr.at[t, d - 1], to_x(d),
            )

    row_of = lax.broadcasted_iota(jnp.int32, (peers * SLOT, node_rows), 1)
    slot_of = lax.broadcasted_iota(jnp.int32, (peers * SLOT, node_rows), 0)
    slot_base = (row_of // rows) * SLOT + row_of % rows

    def node_sum(t):
        v_out = spans_out[t][1] // pieces
        value = xsums[t][xi].astype(F32)
        for d in range(1, xs):
            arrived(xbufs[t].at[d - 1], oxs.at[t, d - 1], oxr.at[t, d - 1], to_x(d))
            value = value + xbufs[t][d - 1].astype(F32)
        value = value.astype(BF16)
        slots = None
        for j in range(pieces):
            gather = jnp.where(slot_of == slot_base + j * rows, 1.0, 0.0).astype(BF16)
            piece = jnp.dot(
                gather, value[:, j * v_out : (j + 1) * v_out], preferred_element_type=F32
            )
            slots = piece if slots is None else slots + piece
        zouts[t][...] = slots.astype(BF16).reshape(peers, SLOT, v_out)
        for d in range(1, peers):
            send(
                zouts[t].at[peer_of(d)], zbufs[t].at[d - 1],
                ozs.at[t, d - 1], ozr.at[t, d - 1], to_peer(d),
            )

    def finish(t):
        at, w_out = spans_out[t]
        v_out = w_out // pieces
        value = zouts[t][p].astype(F32)
        for d in range(1, peers):
            arrived(zbufs[t].at[d - 1], ozs.at[t, d - 1], ozr.at[t, d - 1], to_peer(d))
            value = value + zbufs[t][d - 1].astype(F32)
        for j in range(pieces):
            out_ref[:, at + j * v_out : at + (j + 1) * v_out] = value[
                j * rows : (j + 1) * rows
            ].astype(BF16)

    steps = (second_half, core_sum, node_sum, finish)
    for t in range(chunks_out + LAGS[-1]):
        for lag, step in zip(LAGS, steps):
            if 0 <= t - lag < chunks_out:
                step(t - lag)

    for copy in sends:
        copy.wait_send()


def on_device(moe_rows, route_nodes, gates, w_gate, w_up, w_down):
    node_count = lax.axis_size("node")
    peers = lax.axis_size("peer")
    xs = node_count // CORES
    rows, width = moe_rows.shape
    hidden = w_gate.shape[2]
    pieces = SLOT // rows
    node_rows = peers * rows
    all_rows = node_count * node_rows
    spans_in = chunks_of(width, PARTS_IN)
    spans_out = chunks_of(width, PARTS_OUT)
    ti, to = len(spans_in), len(spans_out)

    vmem = pl.BlockSpec(memory_space=pltpu.VMEM)
    hbm = pl.BlockSpec(memory_space=pl.ANY)
    dma = pltpu.SemaphoreType.DMA
    far = max(peers - 1, 1)
    xfar = max(xs - 1, 1)
    scratch = [
        pltpu.VMEM(w_gate.shape, BF16),
        pltpu.VMEM(w_up.shape, BF16),
        pltpu.VMEM(w_down.shape, BF16),
        [pltpu.VMEM((peers, SLOT, w // pieces), BF16) for _, w in spans_in],
        [pltpu.VMEM((CORES, xs, node_rows, w), BF16) for _, w in spans_in],
        pltpu.VMEM((peers, SLOT, GATE_COLS), BF16),
        pltpu.VMEM((CORES, xs, node_rows, GATE_COLS), BF16),
        pltpu.VMEM((EXP_NODE, 2, all_rows, hidden), F32),
        pltpu.VMEM((EXP_NODE, all_rows, hidden), BF16),
        [pltpu.VMEM((CORES, xs, node_rows, w), BF16) for _, w in spans_out],
        [pltpu.VMEM((xs, node_rows, w), BF16) for _, w in spans_out],
        [pltpu.VMEM((xs, node_rows, w), BF16) for _, w in spans_out],
        [pltpu.VMEM((xfar, node_rows, w), BF16) for _, w in spans_out],
        [pltpu.VMEM((peers, SLOT, w // pieces), BF16) for _, w in spans_out],
        [pltpu.VMEM((far, SLOT, w // pieces), BF16) for _, w in spans_out],
        dma((ti, 2)), dma((to,)),
        dma((ti, far)), dma((ti, far)), dma((ti, xfar)), dma((ti, xfar)),
        dma((ti, xs)), dma((ti, xs)),
        dma((far,)), dma((far,)), dma((xfar,)), dma((xfar,)), dma((xs,)), dma((xs,)),
        dma((to,)), dma((to,)), dma((to, xfar)), dma((to, xfar)), dma((to, far)), dma((to, far)),
    ]
    weight_count = w_gate.size + w_up.size + w_down.size
    return pl.pallas_call(
        functools.partial(kernel, peers, xs, rows, spans_in, spans_out),
        out_shape=jax.ShapeDtypeStruct((rows, width), BF16),
        in_specs=[vmem, vmem, vmem, hbm, hbm, hbm],
        out_specs=vmem,
        scratch_shapes=scratch,
        compiler_params=pltpu.CompilerParams(
            collective_id=0, has_side_effects=True, vmem_limit_bytes=60 * 1024 * 1024
        ),
        cost_estimate=pl.CostEstimate(
            flops=2 * all_rows * weight_count,
            bytes_accessed=2 * weight_count,
            transcendentals=EXP_NODE * all_rows * hidden,
        ),
    )(moe_rows, route_nodes, gates, w_gate, w_up, w_down)


def solution(mesh):
    in_specs = (
        P(("groups", "node", "peer"), None),
        P(("groups", "node", "peer"), None),
        P(("groups", "node", "peer"), None, None),
        P("node", None, "peer"),
        P("node", None, "peer"),
        P("node", "peer", None),
    )
    out_specs = P(("groups", "node", "peer"), None)
    return jax.shard_map(
        on_device, mesh=mesh, in_specs=in_specs, out_specs=out_specs, check_vma=False
    )
```

```python
import functools

import jax
import jax.numpy as jnp
from jax import lax
from jax.experimental import pallas as pl
from jax.experimental.pallas import tpu as pltpu
from jax.sharding import PartitionSpec as P

MESH = pl.DeviceIdType.MESH
EXP_NODE = 2
CORES = 2
SLOT = 16
GATE_COLS = 128
UNIT = 512
PARTS_IN = 7
PARTS_OUT = 4
LAGS = (0, 1, 3, 5)
F32 = jnp.float32
BF16 = jnp.bfloat16


def chunks_of(width, parts):
    units = width // UNIT
    parts = min(parts, units)
    edges = [UNIT * (units * k // parts) for k in range(parts + 1)]
    return [(a, b - a) for a, b in zip(edges[:-1], edges[1:])]


def kernel(
    peers, xs, rows, spans_in, spans_out,
    x_ref, r_ref, g_ref, wg_hbm, wu_hbm, wd_hbm, out_ref,
    wg, wu, wd, zins, gins, zgate, ggate, acc, hid,
    parts, cbufs, xsums, xbufs, zouts, zbufs,
    w_sem, d_sem,
    zs, zr, xs_s, xs_r, cs, cr,
    gzs, gzr, gxs, gxr, gcs, gcr,
    ocs, ocr, oxs, oxr, ozs, ozr,
):
    chunks_in, chunks_out = len(spans_in), len(spans_out)
    pieces = SLOT // rows
    node_rows = peers * rows
    node = lax.axis_index("node")
    p = lax.axis_index("peer")
    c = lax.rem(node, CORES)
    xi = lax.div(node, CORES)

    weight_copies = []
    for t in range(chunks_in):
        both = []
        for i, (src, dst) in enumerate(((wg_hbm, wg), (wu_hbm, wu))):
            span = pl.ds(*spans_in[t])
            copy = pltpu.make_async_copy(src.at[:, span, :], dst.at[:, span, :], w_sem.at[t, i])
            copy.start()
            both.append(copy)
        weight_copies.append(both)
    down_copies = []
    for t in range(chunks_out):
        span = pl.ds(*spans_out[t])
        copy = pltpu.make_async_copy(wd_hbm.at[:, :, span], wd.at[:, :, span], d_sem.at[t])
        copy.start()
        down_copies.append(copy)

    def peer_of(d):
        return lax.rem(p + d, peers)

    def x_of(d):
        return lax.rem(xi + d, xs)

    barrier = pltpu.get_barrier_semaphore()
    for d in range(1, peers):
        pl.semaphore_signal(barrier, inc=1, device_id={"peer": peer_of(d)}, device_id_type=MESH)
    for d in range(1, xs):
        pl.semaphore_signal(
            barrier, inc=1, device_id={"node": x_of(d) * CORES + c}, device_id_type=MESH
        )
    pl.semaphore_signal(
        barrier, inc=1, device_id={"node": xi * CORES + 1 - c}, device_id_type=MESH
    )

    for t in range(chunks_in):
        at, w_in = spans_in[t]
        v_in = w_in // pieces
        own = [
            x_ref[:, at + j * v_in : at + (j + 1) * v_in].astype(F32) for j in range(pieces)
        ]
        zins[t][p] = jnp.concatenate(own, axis=0).astype(BF16)
    column = lax.broadcasted_iota(jnp.int32, (1, GATE_COLS), 1)
    gate_rows = []
    for r in range(rows):
        line = jnp.zeros((1, GATE_COLS), F32)
        values = g_ref[r].astype(F32)
        for j in range(r_ref.shape[1]):
            for e in range(EXP_NODE):
                hit = column == r_ref[r : r + 1, j : j + 1] * EXP_NODE + e
                line = jnp.where(hit, values[j : j + 1, e : e + 1], line)
        gate_rows.append(line)
    zgate[p] = jnp.concatenate(gate_rows * pieces, axis=0).astype(BF16)

    pl.semaphore_wait(barrier, peers - 1 + xs - 1 + 1)

    sends = []

    def send(src, dst, ssem, rsem, where):
        copy = pltpu.make_async_remote_copy(
            src_ref=src, dst_ref=dst, send_sem=ssem, recv_sem=rsem,
            device_id=where, device_id_type=MESH,
        )
        copy.start()
        sends.append(copy)

    def arrived(dst, ssem, rsem, where):
        pltpu.make_async_remote_copy(
            src_ref=dst, dst_ref=dst, send_sem=ssem, recv_sem=rsem,
            device_id=where, device_id_type=MESH,
        ).wait_recv()

    def to_peer(d):
        return {"peer": peer_of(d)}

    def to_x(d):
        return {"node": x_of(d) * CORES + c}

    to_core = {"node": xi * CORES + 1 - c}

    for t in range(chunks_in):
        for d in range(1, peers):
            send(zins[t].at[p], zins[t].at[p], zs.at[t, d - 1], zr.at[t, d - 1], to_peer(d))
    for d in range(1, peers):
        send(zgate.at[p], zgate.at[p], gzs.at[d - 1], gzr.at[d - 1], to_peer(d))

    row_at = lax.broadcasted_iota(jnp.int32, (node_rows, peers * SLOT), 0)
    col_at = lax.broadcasted_iota(jnp.int32, (node_rows, peers * SLOT), 1)
    row_base = (row_at // rows) * SLOT + row_at % rows

    def spread(j):
        return jnp.where(col_at == row_base + j * rows, 1.0, 0.0).astype(BF16)

    def place(t):
        for d in range(1, peers):
            arrived(zins[t].at[peer_of(peers - d)], zs.at[t, d - 1], zr.at[t, d - 1], to_peer(d))
        gin = gins[t]
        v_in = spans_in[t][1] // pieces
        stacked = zins[t][...].reshape(peers * SLOT, v_in)
        for j in range(pieces):
            gin[c, xi, :, j * v_in : (j + 1) * v_in] = jnp.dot(
                spread(j), stacked, preferred_element_type=F32
            ).astype(BF16)
        for d in range(1, xs):
            send(gin.at[c, xi], gin.at[c, xi], xs_s.at[t, d - 1], xs_r.at[t, d - 1], to_x(d))
        send(gin.at[c, xi], gin.at[c, xi], cs.at[t, 0], cr.at[t, 0], to_core)

    def forward(t):
        for d in range(1, xs):
            other = x_of(xs - d)
            block = gins[t].at[c, other]
            arrived(block, xs_s.at[t, d - 1], xs_r.at[t, d - 1], to_x(d))
            send(block, block, cs.at[t, d], cr.at[t, d], to_core)

    def gathered(t):
        for d in range(xs):
            block = gins[t].at[1 - c, x_of(xs - d)]
            arrived(block, cs.at[t, d], cr.at[t, d], to_core)

    all_rows = CORES * xs * node_rows

    def first_half(t):
        gathered(t)
        for copy in weight_copies[t]:
            copy.wait()
        at, w_in = spans_in[t]
        lhs = gins[t][...].reshape(all_rows, w_in)
        for e in range(EXP_NODE):
            for i, w in enumerate((wg, wu)):
                value = jnp.dot(
                    lhs, w[e, at : at + w_in, :], preferred_element_type=F32
                )
                if t == 0:
                    acc[e, i] = value
                else:
                    acc[e, i] += value

    for t in range(chunks_in):
        place(t)

    for d in range(1, peers):
        arrived(zgate.at[peer_of(peers - d)], gzs.at[d - 1], gzr.at[d - 1], to_peer(d))
    ggate[c, xi] = jnp.dot(
        spread(0), zgate[...].reshape(peers * SLOT, GATE_COLS), preferred_element_type=F32
    ).astype(BF16)
    own_gates = ggate.at[c, xi]
    for d in range(1, xs):
        send(own_gates, own_gates, gxs.at[d - 1], gxr.at[d - 1], to_x(d))
    send(own_gates, own_gates, gcs.at[0], gcr.at[0], to_core)

    forward(0)
    for t in range(chunks_in):
        if t + 1 < chunks_in:
            forward(t + 1)
        else:
            for d in range(1, xs):
                block = ggate.at[c, x_of(xs - d)]
                arrived(block, gxs.at[d - 1], gxr.at[d - 1], to_x(d))
                send(block, block, gcs.at[d], gcr.at[d], to_core)
        first_half(t)

    for d in range(xs):
        arrived(ggate.at[1 - c, x_of(xs - d)], gcs.at[d], gcr.at[d], to_core)
    every_gate = ggate[...].reshape(all_rows, GATE_COLS).astype(F32)
    gate_col = lax.broadcasted_iota(jnp.int32, (all_rows, GATE_COLS), 1)
    row_gates = []
    for e in range(EXP_NODE):
        picked = jnp.where(gate_col == node * EXP_NODE + e, every_gate, 0.0)
        row_gates.append(jnp.sum(picked, axis=1, keepdims=True))
        gate_proj = acc[e, 0]
        hid[e] = (gate_proj / (1.0 + jnp.exp(-gate_proj)) * acc[e, 1]).astype(BF16)

    def second_half(t):
        down_copies[t].wait()
        total = None
        at, w_out = spans_out[t]
        for e in range(EXP_NODE):
            value = row_gates[e] * jnp.dot(
                hid[e], wd[e, :, at : at + w_out], preferred_element_type=F32
            )
            total = value if total is None else total + value
        parts[t][...] = total.astype(BF16).reshape(CORES, xs, node_rows, w_out)
        send(parts[t].at[1 - c], cbufs[t], ocs.at[t], ocr.at[t], to_core)

    def core_sum(t):
        arrived(cbufs[t], ocs.at[t], ocr.at[t], to_core)
        xsums[t][...] = (parts[t][c].astype(F32) + cbufs[t][...].astype(F32)).astype(BF16)
        for d in range(1, xs):
            send(
                xsums[t].at[x_of(d)], xbufs[t].at[d - 1],
                oxs.at[t, d - 1], oxr.at[t, d - 1], to_x(d),
            )

    row_of = lax.broadcasted_iota(jnp.int32, (peers * SLOT, node_rows), 1)
    slot_of = lax.broadcasted_iota(jnp.int32, (peers * SLOT, node_rows), 0)
    slot_base = (row_of // rows) * SLOT + row_of % rows

    def node_sum(t):
        v_out = spans_out[t][1] // pieces
        value = xsums[t][xi].astype(F32)
        for d in range(1, xs):
            arrived(xbufs[t].at[d - 1], oxs.at[t, d - 1], oxr.at[t, d - 1], to_x(d))
            value = value + xbufs[t][d - 1].astype(F32)
        value = value.astype(BF16)
        slots = None
        for j in range(pieces):
            gather = jnp.where(slot_of == slot_base + j * rows, 1.0, 0.0).astype(BF16)
            piece = jnp.dot(
                gather, value[:, j * v_out : (j + 1) * v_out], preferred_element_type=F32
            )
            slots = piece if slots is None else slots + piece
        zouts[t][...] = slots.astype(BF16).reshape(peers, SLOT, v_out)
        for d in range(1, peers):
            send(
                zouts[t].at[peer_of(d)], zbufs[t].at[d - 1],
                ozs.at[t, d - 1], ozr.at[t, d - 1], to_peer(d),
            )

    def finish(t):
        at, w_out = spans_out[t]
        v_out = w_out // pieces
        value = zouts[t][p].astype(F32)
        for d in range(1, peers):
            arrived(zbufs[t].at[d - 1], ozs.at[t, d - 1], ozr.at[t, d - 1], to_peer(d))
            value = value + zbufs[t][d - 1].astype(F32)
        for j in range(pieces):
            out_ref[:, at + j * v_out : at + (j + 1) * v_out] = value[
                j * rows : (j + 1) * rows
            ].astype(BF16)

    steps = (second_half, core_sum, node_sum, finish)
    for t in range(chunks_out + LAGS[-1]):
        for lag, step in zip(LAGS, steps):
            if 0 <= t - lag < chunks_out:
                step(t - lag)

    for copy in sends:
        copy.wait_send()


def on_device(moe_rows, route_nodes, gates, w_gate, w_up, w_down):
    node_count = lax.axis_size("node")
    peers = lax.axis_size("peer")
    xs = node_count // CORES
    rows, width = moe_rows.shape
    hidden = w_gate.shape[2]
    pieces = SLOT // rows
    node_rows = peers * rows
    all_rows = node_count * node_rows
    spans_in = chunks_of(width, PARTS_IN)
    spans_out = chunks_of(width, PARTS_OUT)
    ti, to = len(spans_in), len(spans_out)

    vmem = pl.BlockSpec(memory_space=pltpu.VMEM)
    hbm = pl.BlockSpec(memory_space=pl.ANY)
    dma = pltpu.SemaphoreType.DMA
    far = max(peers - 1, 1)
    xfar = max(xs - 1, 1)
    scratch = [
        pltpu.VMEM(w_gate.shape, BF16),
        pltpu.VMEM(w_up.shape, BF16),
        pltpu.VMEM(w_down.shape, BF16),
        [pltpu.VMEM((peers, SLOT, w // pieces), BF16) for _, w in spans_in],
        [pltpu.VMEM((CORES, xs, node_rows, w), BF16) for _, w in spans_in],
        pltpu.VMEM((peers, SLOT, GATE_COLS), BF16),
        pltpu.VMEM((CORES, xs, node_rows, GATE_COLS), BF16),
        pltpu.VMEM((EXP_NODE, 2, all_rows, hidden), F32),
        pltpu.VMEM((EXP_NODE, all_rows, hidden), BF16),
        [pltpu.VMEM((CORES, xs, node_rows, w), BF16) for _, w in spans_out],
        [pltpu.VMEM((xs, node_rows, w), BF16) for _, w in spans_out],
        [pltpu.VMEM((xs, node_rows, w), BF16) for _, w in spans_out],
        [pltpu.VMEM((xfar, node_rows, w), BF16) for _, w in spans_out],
        [pltpu.VMEM((peers, SLOT, w // pieces), BF16) for _, w in spans_out],
        [pltpu.VMEM((far, SLOT, w // pieces), BF16) for _, w in spans_out],
        dma((ti, 2)), dma((to,)),
        dma((ti, far)), dma((ti, far)), dma((ti, xfar)), dma((ti, xfar)),
        dma((ti, xs)), dma((ti, xs)),
        dma((far,)), dma((far,)), dma((xfar,)), dma((xfar,)), dma((xs,)), dma((xs,)),
        dma((to,)), dma((to,)), dma((to, xfar)), dma((to, xfar)), dma((to, far)), dma((to, far)),
    ]
    weight_count = w_gate.size + w_up.size + w_down.size
    return pl.pallas_call(
        functools.partial(kernel, peers, xs, rows, spans_in, spans_out),
        out_shape=jax.ShapeDtypeStruct((rows, width), BF16),
        in_specs=[vmem, vmem, vmem, hbm, hbm, hbm],
        out_specs=vmem,
        scratch_shapes=scratch,
        compiler_params=pltpu.CompilerParams(
            collective_id=0, has_side_effects=True, vmem_limit_bytes=60 * 1024 * 1024
        ),
        cost_estimate=pl.CostEstimate(
            flops=2 * all_rows * weight_count,
            bytes_accessed=2 * weight_count,
            transcendentals=EXP_NODE * all_rows * hidden,
        ),
    )(moe_rows, route_nodes, gates, w_gate, w_up, w_down)


def solution(mesh):
    in_specs = (
        P(("groups", "node", "peer"), None),
        P(("groups", "node", "peer"), None),
        P(("groups", "node", "peer"), None, None),
        P("node", None, "peer"),
        P("node", None, "peer"),
        P("node", "peer", None),
    )
    out_specs = P(("groups", "node", "peer"), None)
    return jax.shard_map(
        on_device, mesh=mesh, in_specs=in_specs, out_specs=out_specs, check_vma=False
    )
```
